128 devices in a mesh: blk: 16 (over x_lo, z, core), head: 8 (over x_hi, y).
Axes of the slice: x: 4 (x_hi: 2, x_lo: 2; x = x_hi * 2 + x_lo), y: 4, z: 4, core: 2. Of those that a mesh axis runs over, the one named last changes fastest.
Arguments:
- queries: bfloat16 [32768, 2048], P(('blk', 'head')), may hold values from -10 to 10
- keys: bfloat16 [32768, 2048], P(('blk', 'head')), may hold values from -3 to 3
- values: bfloat16 [32768, 2048], P(('blk', 'head')), may hold values from -6 to 6
- active: int32 [256, 24], replicated, may hold values from 0 to 255, as said below
Outputs:
- attended: bfloat16 [32768, 2048], P(('blk', 'head'))
The draws below stay inside these ranges and needn't reach their ends.
Inputs may be any that keep to these rules, and one draw needn't show every extreme that they name: `active`: row b lists 24 different key blocks; its first entry is b itself.
All inputs are finite; a program needn't handle non-finite values.
Results may differ from the reference program's by a relative error of at most 0.0047.
Values may be sent and summed in bfloat16 or wider, within the bound.
No kernel may reach another device: no remote copies, remote signals or barrier semaphores. Data moves between devices by JAX's collectives and lax.ppermute only.
A program may use at most 256 MiB of HBM per device.

```python
import math
import jax
import jax.numpy as jnp
from jax import lax

D = 2048
HEADS = 32
HD = 64
BLOCK = 128
ACT = 24
TOKENS = 32768


def draw_keys(key, part):
    key = jax.random.fold_in(key, 2)
    return jnp.clip(jax.random.normal(key, (TOKENS, D), jnp.float32), -3.0, 3.0).astype(jnp.bfloat16)


def draw_queries(key, part):
    key = jax.random.fold_in(key, 1)
    return jnp.clip(jax.random.normal(key, (TOKENS, D), jnp.float32), -6.0, 6.0).astype(jnp.bfloat16)


def draw_active(key, part):
    key = jax.random.fold_in(key, 5)
    blocks = TOKENS // BLOCK
    spacing = max(1, blocks // 16)
    spacing = spacing - 1 + spacing % 2
    spread_count = min(ACT - 2, -(-blocks // spacing))
    extra_count = ACT - 1 - spread_count
    columns = jnp.arange(blocks, dtype=jnp.int32)
    offsets = spacing * jnp.arange(1, spread_count + 1, dtype=jnp.int32)
    spread = (columns[:, None] + offsets[None, :]) % blocks
    noise = jax.random.randint(jax.random.fold_in(key, 1), (blocks, blocks), 0, 1 << 20)
    ranking = noise * blocks + columns[None, :]
    taken = columns[None, :] == columns[:, None]
    taken = taken | jnp.any(spread[:, :, None] == columns[None, None, :], axis=1)
    ranking = jnp.where(taken, -1, ranking)
    unused, picks = lax.top_k(ranking, extra_count)
    return jnp.concatenate([columns[:, None], spread.astype(jnp.int32), picks.astype(jnp.int32)], axis=1).astype(jnp.int32)


def levels(key, shape, split, low, top_value):
    loudness = 1.0
    for dim, blocks in split:
        heights = jax.random.uniform(jax.random.fold_in(jax.random.fold_in(key, 6), dim), (blocks,), jnp.float32, low / len(split), top_value / len(split))
        loudness = loudness * jnp.repeat(jnp.exp(heights), shape[dim] // blocks).reshape((-1,) + (1,) * (len(shape) - 1 - dim))
    return loudness


def scatter_about(rng, extent, width, most, split=(), kind=jnp.bfloat16):
    array = width * jax.random.normal(rng, extent, jnp.float32)
    if split:
        array = array * levels(rng, extent, split, -0.22, 0.18)
    return jnp.clip(array, -most, most).astype(kind)


def setup_inputs(seed: int = 0) -> dict:
    streams_of = jax.random.split(jax.random.key(seed), 5)
    return {
        "queries": draw_queries(jax.random.fold_in(streams_of[4], 71), 0),
        "keys": draw_keys(jax.random.fold_in(streams_of[4], 71), 0),
        "values": scatter_about(streams_of[2], (TOKENS, D), 1.0, 6.0, ((0, 128),)),
        "active": draw_active(jax.random.fold_in(streams_of[4], 71), 0),
    }


def reference(queries, keys, values, active):
    blocks = TOKENS // BLOCK
    scale = 1.0 / math.sqrt(HD)
    q_blocks = queries.reshape(blocks, BLOCK, HEADS, HD)
    k_blocks = keys.reshape(blocks, BLOCK, HEADS, HD)
    v_blocks = values.reshape(blocks, BLOCK, HEADS, HD)

    def one_block(args):
        q_blk, listed = args
        k_sel = jnp.take(k_blocks, listed, axis=0).astype(jnp.float32)
        v_sel = jnp.take(v_blocks, listed, axis=0).astype(jnp.float32)
        scores = jnp.einsum('qhd,akhd->hqak', q_blk.astype(jnp.float32), k_sel) * scale
        top = lax.optimization_barrier(jnp.max(scores, axis=(2, 3), keepdims=True))
        weights = jnp.exp(scores - top)
        total = lax.optimization_barrier(jnp.sum(weights, axis=(2, 3)))
        rounded = lax.optimization_barrier(weights.astype(jnp.bfloat16)).astype(jnp.float32)
        summed = jnp.einsum('hqak,akhd->qhd', rounded, v_sel)
        return (summed / jnp.transpose(total)[:, :, None]).astype(jnp.bfloat16)
    result = lax.map(one_block, (q_blocks, active))
    return result.reshape(TOKENS, D)
```

```python
import functools
import math

import jax
import jax.numpy as jnp
from jax import lax
from jax.experimental import pallas as pl
from jax.experimental.pallas import tpu as pltpu
from jax.sharding import Mesh, PartitionSpec as P

HD = 64
BLOCK = 128
ACT = 24
LIMIT = 2.0**100

AXES = ("near", "z", "core", "far", "y")
HEAD_AXES = ("near", "z", "y")
CHIP_AXES = ("near", "z", "far", "y")


def nt_dot(a, b):
    return lax.dot_general(a, b, (((1,), (1,)), ((), ())), preferred_element_type=jnp.float32)


def swap_halves(x):
    half = x.shape[1] // 2
    return jnp.concatenate([x[:, half:], x[:, :half]], axis=1)


def attend_kernel(place_ref, q_ref, mine_ref, other_ref, o_ref, kk, vt, acc):
    pairs = q_ref.shape[0]
    chunks = mine_ref.shape[0]
    low = lax.broadcasted_iota(jnp.int32, (BLOCK, BLOCK), 1) < HD

    for base, ref in ((0, mine_ref), (2 * chunks, other_ref)):

        @pl.loop(0, chunks)
        def _(c):
            x = ref[c, :BLOCK, :].astype(jnp.float32)
            y = swap_halves(x)
            kk[base + 2 * c] = jnp.where(low, x, y).astype(jnp.bfloat16)
            kk[base + 2 * c + 1] = jnp.where(low, y, x).astype(jnp.bfloat16)
            vt[base + 2 * c] = ref[c, BLOCK : BLOCK + HD, :]
            vt[base + 2 * c + 1] = ref[c, BLOCK + HD :, :]

    ones = jnp.ones((16, 2 * BLOCK), jnp.bfloat16)
    factor = math.log2(math.e) / math.sqrt(HD)

    @pl.loop(0, pairs)
    def _(i):
        q = q_ref[i].astype(jnp.float32) * factor
        high = q.astype(jnp.bfloat16).astype(jnp.float32)
        rest = q - high
        first = jnp.where(low, high, swap_halves(rest)).astype(jnp.bfloat16)
        second = jnp.where(low, swap_halves(high), rest).astype(jnp.bfloat16)
        zero = jnp.zeros_like(first)
        q2 = jnp.concatenate(
            [jnp.concatenate([first, zero], 1), jnp.concatenate([zero, second], 1)], 0
        )

        def scores(t):
            a = place_ref[(2 * i) * ACT + t]
            b = place_ref[(2 * i + 1) * ACT + t]
            return nt_dot(jnp.concatenate([kk[a], kk[b]], axis=1), q2)

        def whole(shift):
            total = [None, None]
            for t in range(0, ACT, 2):
                w = [jnp.exp2(scores(t + n) - shift).astype(jnp.bfloat16) for n in range(2)]
                w = jnp.concatenate(w, axis=0)
                for n in range(2):
                    g = place_ref[(2 * i + n) * ACT + t]
                    h = place_ref[(2 * i + n) * ACT + t + 1]
                    v = jnp.concatenate([vt[g], vt[h]], axis=1)
                    part = jnp.dot(
                        jnp.concatenate([v, ones], axis=0),
                        w[:, n * BLOCK : (n + 1) * BLOCK],
                        preferred_element_type=jnp.float32,
                    )
                    total[n] = part if t == 0 else total[n] + part
            acc[0], acc[1] = total

        whole(jnp.max(scores(0), axis=0, keepdims=True))
        sums = jnp.concatenate([acc[0, HD : HD + 1], acc[1, HD : HD + 1]], axis=1)
        lost = jnp.max(jnp.where(sums <= LIMIT, 0.0, 1.0))

        @pl.when(lost > 0.0)
        def _():
            top = lax.fori_loop(
                0,
                ACT,
                lambda t, m: jnp.maximum(m, jnp.max(scores(t), axis=0, keepdims=True)),
                jnp.full((1, 2 * BLOCK), -jnp.inf, jnp.float32),
            )
            whole(top)

        out = [acc[n, :HD] / acc[n, HD : HD + 1] for n in range(2)]
        o_ref[i] = jnp.transpose(jnp.concatenate(out, axis=0)).astype(jnp.bfloat16)


def attend(place, q, mine, other):
    pairs, chunks = q.shape[0], mine.shape[0]
    vmem = pl.BlockSpec(memory_space=pltpu.VMEM)
    flops = 8 * pairs * ACT * BLOCK * BLOCK * HD
    return pl.pallas_call(
        attend_kernel,
        out_shape=jax.ShapeDtypeStruct(q.shape, jnp.bfloat16),
        in_specs=[pl.BlockSpec(memory_space=pltpu.SMEM), vmem, vmem, vmem],
        out_specs=vmem,
        scratch_shapes=[
            pltpu.VMEM((4 * chunks, BLOCK, BLOCK), jnp.bfloat16),
            pltpu.VMEM((4 * chunks, HD, BLOCK), jnp.bfloat16),
            pltpu.VMEM((2, HD + 16, BLOCK), jnp.float32),
        ],
        compiler_params=pltpu.CompilerParams(vmem_limit_bytes=52 * 2**20),
        cost_estimate=pl.CostEstimate(
            flops=flops, bytes_accessed=10 * 2**20, transcendentals=2 * pairs * ACT * BLOCK * BLOCK
        ),
    )(place, q, mine, other)


def on_device(queries, keys, values, active):
    near, z, far, y = (lax.axis_size(a) for a in CHIP_AXES)
    heads = near * z * y
    blocks = queries.shape[0] // BLOCK
    core, far_id = lax.axis_index("core"), lax.axis_index("far")

    def side_by_side(x):
        x = x.reshape(blocks, BLOCK, heads, HD)
        return jnp.transpose(x, (2, 1, 0, 3)).reshape(heads, BLOCK, blocks * HD)

    q = side_by_side(queries)
    k = side_by_side(keys)
    v = jnp.transpose(values.reshape(blocks, BLOCK, heads, HD), (2, 0, 3, 1))
    v = v.reshape(heads, blocks * HD, BLOCK)
    kv = jnp.concatenate([k, v], axis=1).reshape(near, z, 1, y, 2 * BLOCK, BLOCK)
    kv = jnp.broadcast_to(kv, (near, z, far, y, 2 * BLOCK, BLOCK))
    kv = kv.reshape(near * z * far * y, 2 * BLOCK, BLOCK)

    q = lax.all_to_all(q, HEAD_AXES, 0, 0, tiled=True)
    mine = lax.all_to_all(kv, CHIP_AXES, 0, 0, tiled=True)
    other = lax.ppermute(mine, "core", [(0, 1), (1, 0)])

    per_core = far * y * blocks
    table = active.reshape(near * z, 2, far, y, blocks, ACT)
    table = lax.dynamic_slice(
        table, (0, core, far_id, 0, 0, 0), (near * z, 1, 1, y, blocks, ACT)
    ).reshape(-1)
    of_other = ((table // per_core) % 2) != core
    place = table // (2 * per_core) * per_core + table % per_core
    place = place + jnp.where(of_other, near * z * per_core, 0)

    out = attend(place, q, mine, other)
    out = lax.all_to_all(out, HEAD_AXES, 0, 0, tiled=True)
    out = out.reshape(heads, BLOCK, blocks, HD)
    return jnp.transpose(out, (2, 1, 0, 3)).reshape(queries.shape)


def solution(mesh):
    fine = Mesh(mesh.devices.reshape(2, 4, 2, 2, 4), AXES)
    tokens = P(AXES, None)
    return jax.shard_map(
        on_device,
        mesh=fine,
        in_specs=(tokens, tokens, tokens, P()),
        out_specs=tokens,
        check_vma=False,
    )
```

```python
import functools
import math

import jax
import jax.numpy as jnp
from jax import lax
from jax.experimental import pallas as pl
from jax.experimental.pallas import tpu as pltpu
from jax.sharding import Mesh, PartitionSpec as P

HD = 64
BLOCK = 128
ACT = 24
LIMIT = 2.0**100

AXES = ("near", "z", "core", "far", "y")
HEAD_AXES = ("near", "z", "y")
CHIP_AXES = ("near", "z", "far", "y")


def swap_halves(x):
    half = x.shape[1] // 2
    return jnp.concatenate([x[:, half:], x[:, :half]], axis=1)


def attend_kernel(
    place_ref, q_ref, mine_ref, other_ref, o_ref, kp, kk, vt, q2, shift, sums, sems
):
    pairs = q_ref.shape[0]
    chunks = mine_ref.shape[0]
    low = lax.broadcasted_iota(jnp.int32, (BLOCK, BLOCK), 1) < HD

    copies = []
    for n, ref in enumerate((mine_ref, other_ref)):
        there = pl.ds(n * chunks, chunks)
        copies.append(pltpu.make_async_copy(ref.at[:, :BLOCK, :], kp.at[there], sems.at[n]))
        copies.append(pltpu.make_async_copy(ref.at[:, BLOCK:, :], vt.at[there], sems.at[2 + n]))
    for copy in copies:
        copy.start()

    for n in range(2):
        copies[2 * n].wait()

        @pl.loop(n * chunks, (n + 1) * chunks, step=8)
        def _(first):
            for c in [first + u for u in range(8)]:
                x = kp[c]
                y = swap_halves(x)
                kk[2 * c] = jnp.where(low, x, y)
                kk[2 * c + 1] = jnp.where(low, y, x)

    def scores(i, t, n):
        rows = []
        for j in range(t, t + n):
            a = place_ref[2 * i * ACT + j]
            b = place_ref[(2 * i + 1) * ACT + j]
            rows.append(jnp.concatenate([kk[a], kk[b]], axis=1))
        return jnp.dot(
            jnp.concatenate(rows, axis=0), q2[i], preferred_element_type=jnp.float32
        )

    def scores_at(i, t):
        a = place_ref[2 * i * ACT + t]
        b = place_ref[(2 * i + 1) * ACT + t]
        x = jnp.concatenate([kk[a], kk[b]], axis=1)
        return jnp.dot(x, q2[i], preferred_element_type=jnp.float32)

    factor = math.log2(math.e) / math.sqrt(HD)

    @pl.loop(0, pairs, step=4)
    def _(first):
        for i in [first + u for u in range(4)]:
            q = q_ref[i].astype(jnp.float32) * factor
            high = q.astype(jnp.bfloat16).astype(jnp.float32)
            rest = q - high
            a = jnp.transpose(jnp.where(low, high, swap_halves(rest)))
            b = jnp.transpose(jnp.where(low, swap_halves(high), rest))
            zero = jnp.zeros((BLOCK, BLOCK), jnp.bfloat16)
            q2[i, :BLOCK, :BLOCK] = a.astype(jnp.bfloat16)
            q2[i, :BLOCK, BLOCK:] = zero
            q2[i, BLOCK:, :BLOCK] = zero
            q2[i, BLOCK:, BLOCK:] = b.astype(jnp.bfloat16)
        for i in [first + u for u in range(4)]:
            shift[i] = jnp.max(scores(i, 0, 1), axis=0, keepdims=True)

    for n in range(2):
        copies[2 * n + 1].wait()

    def values(i, n, t, count):
        blocks = []
        for j in range(t, t + count):
            g = place_ref[(2 * i + n) * ACT + j]
            blocks.append(vt[g // 2, pl.ds(pl.multiple_of((g % 2) * HD, HD), HD), :])
        return jnp.concatenate(blocks, axis=1)

    def whole(i, count):
        ones = jnp.ones((16, count * BLOCK), jnp.bfloat16)
        total = None
        for t in range(0, ACT, count):
            w = jnp.exp2(scores(i, t, count) - shift[i]).astype(jnp.bfloat16)
            v = jnp.concatenate([values(i, 0, t, count), values(i, 1, t, count), ones], axis=0)
            part = jnp.dot(v, w, preferred_element_type=jnp.float32)
            total = part if total is None else total + part
        sums[i] = total[2 * HD : 2 * HD + 1]
        inverse = 1.0 / sums[i]
        out = jnp.concatenate(
            [
                total[:HD, :BLOCK] * inverse[:, :BLOCK],
                total[HD : 2 * HD, BLOCK:] * inverse[:, BLOCK:],
            ],
            axis=0,
        )
        o_ref[i] = jnp.transpose(out).astype(jnp.bfloat16)

    @pl.loop(0, pairs, step=4)
    def _(first):
        for u in range(4):
            whole(first + u, 8)

    def lost(s):
        return jnp.max(jnp.where(s <= LIMIT, 0.0, 1.0)) > 0.0

    @pl.when(lost(sums[...]))
    def _():
        @pl.loop(0, pairs)
        def _(i):
            @pl.when(lost(sums[i]))
            def _():
                shift[i] = lax.fori_loop(
                    0,
                    ACT,
                    lambda t, top: jnp.maximum(
                        top, jnp.max(scores_at(i, t), axis=0, keepdims=True)
                    ),
                    jnp.full((1, 2 * BLOCK), -jnp.inf, jnp.float32),
                )
                whole(i, 2)


def attend(place, q, mine, other):
    pairs, chunks = q.shape[0], mine.shape[0]
    vmem = pl.BlockSpec(memory_space=pltpu.VMEM)
    anywhere = pl.BlockSpec(memory_space=pl.ANY)
    return pl.pallas_call(
        attend_kernel,
        out_shape=jax.ShapeDtypeStruct(q.shape, jnp.bfloat16),
        in_specs=[pl.BlockSpec(memory_space=pltpu.SMEM), vmem, anywhere, anywhere],
        out_specs=vmem,
        scratch_shapes=[
            pltpu.VMEM((2 * chunks, BLOCK, BLOCK), jnp.bfloat16),
            pltpu.VMEM((4 * chunks, BLOCK, BLOCK), jnp.bfloat16),
            pltpu.VMEM((2 * chunks, BLOCK, BLOCK), jnp.bfloat16),
            pltpu.VMEM((pairs, 2 * BLOCK, 2 * BLOCK), jnp.bfloat16),
            pltpu.VMEM((pairs, 1, 2 * BLOCK), jnp.float32),
            pltpu.VMEM((pairs, 1, 2 * BLOCK), jnp.float32),
            pltpu.SemaphoreType.DMA((4,)),
        ],
        compiler_params=pltpu.CompilerParams(vmem_limit_bytes=48 * 2**20),
        cost_estimate=pl.CostEstimate(
            flops=8 * pairs * ACT * BLOCK * BLOCK * HD,
            bytes_accessed=10 * 2**20,
            transcendentals=2 * pairs * ACT * BLOCK * BLOCK,
        ),
    )(place, q, mine, other)


def on_device(queries, keys, values, active):
    near, z, far, y = (lax.axis_size(a) for a in CHIP_AXES)
    heads = near * z * y
    blocks = queries.shape[0] // BLOCK
    core, far_id = lax.axis_index("core"), lax.axis_index("far")

    def side_by_side(x):
        x = x.reshape(blocks, BLOCK, heads, HD)
        return jnp.transpose(x, (2, 1, 0, 3)).reshape(heads, BLOCK, blocks * HD)

    q = side_by_side(queries)
    k = side_by_side(keys)
    v = jnp.transpose(values.reshape(blocks, BLOCK, heads, HD), (2, 0, 3, 1))
    v = v.reshape(heads, blocks * HD, BLOCK)
    kv = jnp.concatenate([k, v], axis=1).reshape(near, z, 1, y, 2 * BLOCK, BLOCK)
    kv = jnp.broadcast_to(kv, (near, z, far, y, 2 * BLOCK, BLOCK))
    kv = kv.reshape(near * z * far * y, 2 * BLOCK, BLOCK)

    q = lax.all_to_all(q, HEAD_AXES, 0, 0, tiled=True)
    mine = lax.all_to_all(kv, CHIP_AXES, 0, 0, tiled=True)
    other = lax.ppermute(mine, "core", [(0, 1), (1, 0)])

    per_core = far * y * blocks
    table = active.reshape(near * z, 2, far, y, blocks, ACT)
    table = lax.dynamic_slice(
        table, (0, core, far_id, 0, 0, 0), (near * z, 1, 1, y, blocks, ACT)
    ).reshape(-1)
    of_other = ((table // per_core) % 2) != core
    place = table // (2 * per_core) * per_core + table % per_core
    place = place + jnp.where(of_other, near * z * per_core, 0)

    out = attend(place, q, mine, other)
    out = lax.all_to_all(out, HEAD_AXES, 0, 0, tiled=True)
    out = out.reshape(heads, BLOCK, blocks, HD)
    return jnp.transpose(out, (2, 1, 0, 3)).reshape(queries.shape)


def solution(mesh):
    fine = Mesh(mesh.devices.reshape(2, 4, 2, 2, 4), AXES)
    tokens = P(AXES, None)
    return jax.shard_map(
        on_device,
        mesh=fine,
        in_specs=(tokens, tokens, tokens, P()),
        out_specs=tokens,
        check_vma=False,
    )
```

```python
import functools
import math

import jax
import jax.numpy as jnp
from jax import lax
from jax.experimental import pallas as pl
from jax.experimental.pallas import tpu as pltpu
from jax.sharding import Mesh, PartitionSpec as P

HD = 64
BLOCK = 128
ACT = 24
LIMIT = 2.0**100

AXES = ("near", "z", "core", "far", "y")
HEAD_AXES = ("near", "z", "y")
CHIP_AXES = ("near", "z", "far", "y")


def swap_halves(x):
    half = x.shape[1] // 2
    return jnp.concatenate([x[:, half:], x[:, :half]], axis=1)


def both_blocks(x):
    low = lax.broadcasted_iota(jnp.int32, (BLOCK, 2 * HD), 1) < HD
    top, bottom = x[:BLOCK], x[BLOCK:]
    return jnp.where(low, top, swap_halves(bottom)), jnp.where(low, swap_halves(top), bottom)


def pack_kernel(q_ref, k_ref, v_ref, q_out, kv_out):
    for pair in range(q_out.shape[0] // 2):
        columns = pl.ds(pair * 2 * HD, 2 * HD)
        for n, block in enumerate(both_blocks(q_ref[:, columns])):
            q_out[2 * pair + n] = block
        keys = both_blocks(k_ref[:, columns])
        v = jnp.transpose(v_ref[:, columns])
        for n in range(2):
            rows = v[n * HD : (n + 1) * HD]
            for copy in range(kv_out.shape[1]):
                kv_out[0, copy, 2 * pair + n, :BLOCK] = keys[n]
                kv_out[0, copy, 2 * pair + n, BLOCK : BLOCK + HD] = rows[:, :BLOCK]
                kv_out[0, copy, 2 * pair + n, BLOCK + HD :] = rows[:, BLOCK:]


def pack(queries, keys, values, groups, copies, heads):
    rows, width = queries.shape
    block = pl.BlockSpec((rows, width // groups), lambda g: (0, g))
    return pl.pallas_call(
        pack_kernel,
        grid=(groups,),
        out_shape=(
            jax.ShapeDtypeStruct((groups * heads, BLOCK, 2 * HD), queries.dtype),
            jax.ShapeDtypeStruct((groups, copies, heads, 2 * BLOCK, BLOCK), keys.dtype),
        ),
        in_specs=[block] * 3,
        out_specs=(
            pl.BlockSpec((heads, BLOCK, 2 * HD), lambda g: (g, 0, 0)),
            pl.BlockSpec((1, copies, heads, 2 * BLOCK, BLOCK), lambda g: (g, 0, 0, 0, 0)),
        ),
    )(queries, keys, values)


def unpack_kernel(x_ref, o_ref):
    low = lax.broadcasted_iota(jnp.int32, (BLOCK, 2 * HD), 1) < HD
    for pair in range(x_ref.shape[0] // 2):
        columns = pl.ds(pair * 2 * HD, 2 * HD)
        x, y = x_ref[2 * pair], x_ref[2 * pair + 1]
        o_ref[:BLOCK, columns] = jnp.where(low, x, swap_halves(y))
        o_ref[BLOCK:, columns] = jnp.where(low, swap_halves(x), y)


def unpack(x, groups):
    heads = x.shape[0]
    return pl.pallas_call(
        unpack_kernel,
        grid=(groups,),
        out_shape=jax.ShapeDtypeStruct((2 * BLOCK, heads * HD), x.dtype),
        in_specs=[pl.BlockSpec((heads // groups, BLOCK, 2 * HD), lambda g: (g, 0, 0))],
        out_specs=pl.BlockSpec((2 * BLOCK, heads * HD // groups), lambda g: (0, g)),
    )(x)


def attend_kernel(
    place_ref, q_ref, mine_ref, other_ref, o_ref, kk, vt, q2, shift, sums, sems
):
    pairs = q_ref.shape[0]
    chunks = mine_ref.shape[0]
    low = lax.broadcasted_iota(jnp.int32, (BLOCK, BLOCK), 1) < HD

    keys, rest = [], []
    for n, ref in enumerate((mine_ref, other_ref)):
        first, second = pl.ds(n * chunks, chunks), pl.ds((2 + n) * chunks, chunks)
        sem = sems.at[n]
        keys.append(pltpu.make_async_copy(ref.at[:, :BLOCK, :], kk.at[first], sem.at[0]))
        upper, lower = ref.at[:, BLOCK : BLOCK + HD, :], ref.at[:, BLOCK + HD :, :]
        rest.append(pltpu.make_async_copy(upper, vt.at[first], sem.at[1]))
        rest.append(pltpu.make_async_copy(lower, vt.at[second], sem.at[2]))
    for copy in keys + rest:
        copy.start()

    for n in range(2):
        keys[n].wait()

        @pl.loop(n * chunks, (n + 1) * chunks, step=8)
        def _(first):
            for c in [first + u for u in range(8)]:
                kk[2 * chunks + c] = swap_halves(kk[c])

    def scores(i, t, n):
        rows = []
        for j in range(n):
            a = place_ref[2 * i * ACT + t + j]
            b = place_ref[(2 * (pairs + i) + 1) * ACT + t + j]
            rows.append(jnp.where(low, kk[a], kk[b]))
        rows = jnp.concatenate(rows, axis=0) if n > 1 else rows[0]
        return jnp.dot(rows, q2[i], preferred_element_type=jnp.float32)

    factor = math.log2(math.e) / math.sqrt(HD)

    @pl.loop(0, pairs, step=4)
    def _(first):
        for i in [first + u for u in range(4)]:
            q = jnp.transpose(q_ref[i].astype(jnp.float32)).astype(jnp.bfloat16)
            zero = jnp.zeros((HD, BLOCK), jnp.bfloat16)
            q2[i, :HD, :BLOCK] = q[:HD]
            q2[i, :HD, BLOCK:] = zero
            q2[i, HD:, :BLOCK] = zero
            q2[i, HD:, BLOCK:] = q[HD:]
        for i in [first + u for u in range(4)]:
            shift[i] = factor * jnp.max(scores(i, 0, 1), axis=0, keepdims=True)

    for copy in rest:
        copy.wait()

    def values(i, n, t, count):
        blocks = [vt[place_ref[(2 * i + n) * ACT + t + j]] for j in range(count)]
        return jnp.concatenate(blocks, axis=1)

    def weights(i, s):
        return jnp.exp2(s * factor - shift[i]).astype(jnp.bfloat16)

    def weighted(i, t, w, count):
        ones = jnp.ones((16, count * BLOCK), jnp.bfloat16)
        v = jnp.concatenate([values(i, 0, t, count), values(i, 1, t, count), ones], axis=0)
        return jnp.dot(v, w, preferred_element_type=jnp.float32)

    def finish(i, total):
        sums[i] = total[2 * HD : 2 * HD + 1]
        inverse = 1.0 / sums[i]
        out = jnp.concatenate(
            [
                total[:HD, :BLOCK] * inverse[:, :BLOCK],
                total[HD : 2 * HD, BLOCK:] * inverse[:, BLOCK:],
            ],
            axis=0,
        )
        o_ref[i] = jnp.transpose(out).astype(jnp.bfloat16)

    def run(todo, count):
        steps = [(i, t) for i in todo for t in range(0, ACT, count)]
        score, weight, total = {}, {}, None
        for k in range(len(steps) + 2):
            if k < len(steps):
                score[k] = scores(*steps[k], count)
            if 0 < k <= len(steps):
                weight[k - 1] = weights(steps[k - 1][0], score.pop(k - 1))
            if 1 < k:
                i, t = steps[k - 2]
                part = weighted(i, t, weight.pop(k - 2), count)
                total = part if t == 0 else total + part
                if t + count == ACT:
                    finish(i, total)

    @pl.loop(0, pairs, step=4)
    def _(first):
        run([first + u for u in range(4)], 4)

    def lost(s):
        return jnp.max(jnp.where(s <= LIMIT, 0.0, 1.0)) > 0.0

    @pl.when(lost(sums[...]))
    def _():
        @pl.loop(0, pairs)
        def _(i):
            @pl.when(lost(sums[i]))
            def _():
                def higher(t, top):
                    return jnp.maximum(top, jnp.max(scores(i, t, 1), axis=0, keepdims=True))

                lowest = jnp.full((1, 2 * BLOCK), -jnp.inf, jnp.float32)
                shift[i] = factor * lax.fori_loop(0, ACT, higher, lowest)
                run([i], 2)


def attend(place, q, mine, other):
    pairs, chunks = q.shape[0], mine.shape[0]
    vmem = pl.BlockSpec(memory_space=pltpu.VMEM)
    anywhere = pl.BlockSpec(memory_space=pl.ANY)
    return pl.pallas_call(
        attend_kernel,
        out_shape=jax.ShapeDtypeStruct(q.shape, jnp.bfloat16),
        in_specs=[pl.BlockSpec(memory_space=pltpu.SMEM), vmem, anywhere, anywhere],
        out_specs=vmem,
        scratch_shapes=[
            pltpu.VMEM((4 * chunks, BLOCK, BLOCK), jnp.bfloat16),
            pltpu.VMEM((4 * chunks, HD, BLOCK), jnp.bfloat16),
            pltpu.VMEM((pairs, BLOCK, 2 * BLOCK), jnp.bfloat16),
            pltpu.VMEM((pairs, 1, 2 * BLOCK), jnp.float32),
            pltpu.VMEM((pairs, 1, 2 * BLOCK), jnp.float32),
            pltpu.SemaphoreType.DMA((2, 3)),
        ],
        compiler_params=pltpu.CompilerParams(vmem_limit_bytes=48 * 2**20),
        cost_estimate=pl.CostEstimate(
            flops=8 * pairs * ACT * BLOCK * BLOCK * HD,
            bytes_accessed=10 * 2**20,
            transcendentals=2 * pairs * ACT * BLOCK * BLOCK,
        ),
    )(place, q, mine, other)


def on_device(queries, keys, values, active):
    near, z, far, y = (lax.axis_size(a) for a in CHIP_AXES)
    heads = near * z * y
    blocks = queries.shape[0] // BLOCK
    core, far_id = lax.axis_index("core"), lax.axis_index("far")

    q, kv = pack(queries, keys, values, near * z, far, y)
    kv = kv.reshape(near * z * far * y, 2 * BLOCK, BLOCK)

    q = lax.all_to_all(q, HEAD_AXES, 0, 0, tiled=True)
    mine = lax.all_to_all(kv, CHIP_AXES, 0, 0, tiled=True)
    other = lax.ppermute(mine, "core", [(0, 1), (1, 0)])

    per_core = far * y * blocks
    chunks = near * z * far * y
    table = active.reshape(near * z, 2, far, y, blocks, ACT)
    table = lax.dynamic_slice(
        table, (0, core, far_id, 0, 0, 0), (near * z, 1, 1, y, blocks, ACT)
    ).reshape(-1)
    of_other = ((table // per_core) % 2) != core
    chunk = (table // (2 * per_core) * per_core + table % per_core) // 2
    chunk = chunk + jnp.where(of_other, chunks, 0)
    place = jnp.concatenate(
        [chunk + 2 * chunks * (table % 2), chunk + 2 * chunks * (1 - table % 2)]
    )

    out = attend(place, q, mine, other)
    out = lax.all_to_all(out, HEAD_AXES, 0, 0, tiled=True)
    return unpack(out, near * z)


def solution(mesh):
    fine = Mesh(mesh.devices.reshape(2, 4, 2, 2, 4), AXES)
    tokens = P(AXES, None)
    return jax.shard_map(
        on_device,
        mesh=fine,
        in_specs=(tokens, tokens, tokens, P()),
        out_specs=tokens,
        check_vma=False,
    )
```

```python
import functools
import math

import jax
import jax.numpy as jnp
from jax import lax
from jax.experimental import pallas as pl
from jax.experimental.pallas import tpu as pltpu
from jax.sharding import Mesh, PartitionSpec as P

HD = 64
BLOCK = 128
ACT = 24
LIMIT = 2.0**100
KEY_COPIES = 4

AXES = ("near", "z", "core", "far", "y")
HEAD_AXES = ("z", "near", "y")
CHIP_AXES = ("z", "near", "y", "far")


def swap_halves(x):
    half = x.shape[1] // 2
    return jnp.concatenate([x[:, half:], x[:, :half]], axis=1)


def both_blocks(x):
    low = lax.broadcasted_iota(jnp.int32, (BLOCK, 2 * HD), 1) < HD
    top, bottom = x[:BLOCK], x[BLOCK:]
    return jnp.where(low, top, swap_halves(bottom)), jnp.where(low, swap_halves(top), bottom)


def pack_kernel(q_ref, k_ref, v_ref, q_out, kv_out, q, k, v, q_new, kv_new, came, gone):
    heads, copies = kv_out.shape[:2]
    parts = came.shape[0]
    width = q.shape[1] // parts
    share = heads // parts
    arrivals = []
    for part in range(parts):
        columns = pl.ds(part * width, width)
        arrivals.append(
            [
                pltpu.make_async_copy(there.at[:, columns], here.at[:, columns], came.at[part, n])
                for n, (there, here) in enumerate(((k_ref, k), (v_ref, v), (q_ref, q)))
            ]
        )
        for copy in arrivals[part]:
            copy.start()
    departures = []
    for part in range(parts):
        for copy in arrivals[part]:
            copy.wait()
        for pair in range(part * width // (2 * HD), (part + 1) * width // (2 * HD)):
            columns = pl.ds(pair * 2 * HD, 2 * HD)
            keys = both_blocks(k[:, columns])
            queries = both_blocks(q[:, columns])
            values = jnp.transpose(v[:, columns])
            for n in range(2):
                rows = values[n * HD : (n + 1) * HD]
                q_new[2 * pair + n] = queries[n]
                kv_new[2 * pair + n, :BLOCK] = keys[n]
                kv_new[2 * pair + n, BLOCK : BLOCK + HD] = rows[:, :BLOCK]
                kv_new[2 * pair + n, BLOCK + HD :] = rows[:, BLOCK:]
        here = pl.ds(part * share, share)
        for n in range(copies):
            departures.append(
                pltpu.make_async_copy(kv_new.at[here], kv_out.at[here, n], gone.at[part, n])
            )
        departures.append(
            pltpu.make_async_copy(q_new.at[here], q_out.at[here], gone.at[part, copies])
        )
        for copy in departures[-copies - 1 :]:
            copy.start()
    for copy in departures:
        copy.wait()


def pack(queries, keys, values, heads, copies, parts):
    anywhere = pl.BlockSpec(memory_space=pl.ANY)
    whole = pltpu.VMEM(queries.shape, queries.dtype)
    return pl.pallas_call(
        pack_kernel,
        out_shape=(
            jax.ShapeDtypeStruct((heads, BLOCK, 2 * HD), queries.dtype),
            jax.ShapeDtypeStruct((heads, copies, 2 * BLOCK, BLOCK), keys.dtype),
        ),
        in_specs=[anywhere] * 3,
        out_specs=(anywhere, anywhere),
        scratch_shapes=[whole] * 3
        + [
            pltpu.VMEM((heads, BLOCK, 2 * HD), queries.dtype),
            pltpu.VMEM((heads, 2 * BLOCK, BLOCK), keys.dtype),
            pltpu.SemaphoreType.DMA((parts, 3)),
            pltpu.SemaphoreType.DMA((parts, copies + 1)),
        ],
        compiler_params=pltpu.CompilerParams(vmem_limit_bytes=63 * 2**20),
    )(queries, keys, values)


def unpack_kernel(x_ref, o_ref):
    low = lax.broadcasted_iota(jnp.int32, (BLOCK, 2 * HD), 1) < HD
    for pair in range(x_ref.shape[0] // 2):
        columns = pl.ds(pair * 2 * HD, 2 * HD)
        x, y = x_ref[2 * pair], x_ref[2 * pair + 1]
        o_ref[:BLOCK, columns] = jnp.where(low, x, swap_halves(y))
        o_ref[BLOCK:, columns] = jnp.where(low, swap_halves(x), y)


def unpack(x, groups):
    heads = x.shape[0]
    return pl.pallas_call(
        unpack_kernel,
        grid=(groups,),
        out_shape=jax.ShapeDtypeStruct((2 * BLOCK, heads * HD), x.dtype),
        in_specs=[pl.BlockSpec((heads // groups, BLOCK, 2 * HD), lambda g: (g, 0, 0))],
        out_specs=pl.BlockSpec((2 * BLOCK, heads * HD // groups), lambda g: (0, g)),
    )(x)


def attend_kernel(
    place_ref, q_ref, mine_ref, other_ref, o_ref, kk, vt, q2, shift, sums, sems
):
    pairs = q_ref.shape[0]
    chunks = mine_ref.shape[0]
    low = lax.broadcasted_iota(jnp.int32, (BLOCK, BLOCK), 1) < HD

    keys, rest = [], []
    piece = chunks // KEY_COPIES
    for n, ref in enumerate((mine_ref, other_ref)):
        for part in range(KEY_COPIES):
            there, here = pl.ds(part * piece, piece), pl.ds(n * chunks + part * piece, piece)
            copy = pltpu.make_async_copy(
                ref.at[there, :BLOCK, :], kk.at[here], sems.at[n, part]
            )
            keys.append((copy, n * chunks + part * piece))
        for side in range(2):
            here = pl.ds((2 * side + n) * chunks, chunks)
            rows = ref.at[:, BLOCK + side * HD : BLOCK + (side + 1) * HD, :]
            rest.append(
                pltpu.make_async_copy(rows, vt.at[here], sems.at[n, KEY_COPIES + side])
            )
    for copy, _ in keys:
        copy.start()
    for copy in rest:
        copy.start()

    @pl.loop(0, pairs, step=4)
    def _(first):
        for i in [first + u for u in range(4)]:
            q = jnp.transpose(q_ref[i].astype(jnp.float32)).astype(jnp.bfloat16)
            zero = jnp.zeros((HD, BLOCK), jnp.bfloat16)
            q2[i, :HD, :BLOCK] = q[:HD]
            q2[i, :HD, BLOCK:] = zero
            q2[i, HD:, :BLOCK] = zero
            q2[i, HD:, BLOCK:] = q[HD:]

    for copy, begin in keys:
        copy.wait()

        @pl.loop(begin, begin + piece, step=8)
        def _(first):
            for c in [first + u for u in range(8)]:
                kk[2 * chunks + c] = swap_halves(kk[c])

    def scores(i, t, n):
        rows = []
        for j in range(n):
            a = place_ref[2 * i * ACT + t + j]
            b = place_ref[(2 * (pairs + i) + 1) * ACT + t + j]
            rows.append(jnp.where(low, kk[a], kk[b]))
        rows = jnp.concatenate(rows, axis=0) if n > 1 else rows[0]
        return jnp.dot(rows, q2[i], preferred_element_type=jnp.float32)

    factor = math.log2(math.e) / math.sqrt(HD)

    @pl.loop(0, pairs, step=8)
    def _(first):
        for i in [first + u for u in range(8)]:
            shift[i] = factor * jnp.max(scores(i, 0, 1), axis=0, keepdims=True)

    for copy in rest:
        copy.wait()

    def values(i, n, t, count):
        blocks = [vt[place_ref[(2 * i + n) * ACT + t + j]] for j in range(count)]
        return jnp.concatenate(blocks, axis=1)

    def weights(i, s):
        return jnp.exp2(s * factor - shift[i]).astype(jnp.bfloat16)

    def weighted(i, t, w, count):
        ones = jnp.ones((16, count * BLOCK), jnp.bfloat16)
        v = jnp.concatenate([values(i, 0, t, count), values(i, 1, t, count), ones], axis=0)
        return jnp.dot(v, w, preferred_element_type=jnp.float32)

    def finish(i, total):
        sums[i] = total[2 * HD : 2 * HD + 1]
        inverse = 1.0 / sums[i]
        out = jnp.concatenate(
            [
                total[:HD, :BLOCK] * inverse[:, :BLOCK],
                total[HD : 2 * HD, BLOCK:] * inverse[:, BLOCK:],
            ],
            axis=0,
        )
        o_ref[i] = jnp.transpose(out).astype(jnp.bfloat16)

    def run(todo, count):
        steps = [(i, t) for i in todo for t in range(0, ACT, count)]
        score, weight, total = {}, {}, None
        for k in range(len(steps) + 2):
            if k < len(steps):
                score[k] = scores(*steps[k], count)
            if 0 < k <= len(steps):
                weight[k - 1] = weights(steps[k - 1][0], score.pop(k - 1))
            if 1 < k:
                i, t = steps[k - 2]
                part = weighted(i, t, weight.pop(k - 2), count)
                total = part if t == 0 else total + part
                if t + count == ACT:
                    finish(i, total)

    @pl.loop(0, pairs, step=8)
    def _(first):
        run([first + u for u in range(8)], 4)

    def lost(s):
        return jnp.max(jnp.where(s <= LIMIT, 0.0, 1.0)) > 0.0

    @pl.when(lost(sums[...]))
    def _():
        @pl.loop(0, pairs)
        def _(i):
            @pl.when(lost(sums[i]))
            def _():
                def higher(t, top):
                    return jnp.maximum(top, jnp.max(scores(i, t, 1), axis=0, keepdims=True))

                lowest = jnp.full((1, 2 * BLOCK), -jnp.inf, jnp.float32)
                shift[i] = factor * lax.fori_loop(0, ACT, higher, lowest)
                run([i], 2)


def attend(place, q, mine, other):
    pairs, chunks = q.shape[0], mine.shape[0]
    vmem = pl.BlockSpec(memory_space=pltpu.VMEM)
    anywhere = pl.BlockSpec(memory_space=pl.ANY)
    return pl.pallas_call(
        attend_kernel,
        out_shape=jax.ShapeDtypeStruct(q.shape, jnp.bfloat16),
        in_specs=[pl.BlockSpec(memory_space=pltpu.SMEM), vmem, anywhere, anywhere],
        out_specs=vmem,
        scratch_shapes=[
            pltpu.VMEM((4 * chunks, BLOCK, BLOCK), jnp.bfloat16),
            pltpu.VMEM((4 * chunks, HD, BLOCK), jnp.bfloat16),
            pltpu.VMEM((pairs, BLOCK, 2 * BLOCK), jnp.bfloat16),
            pltpu.VMEM((pairs, 1, 2 * BLOCK), jnp.float32),
            pltpu.VMEM((pairs, 1, 2 * BLOCK), jnp.float32),
            pltpu.SemaphoreType.DMA((2, KEY_COPIES + 2)),
        ],
        compiler_params=pltpu.CompilerParams(vmem_limit_bytes=48 * 2**20),
        cost_estimate=pl.CostEstimate(
            flops=8 * pairs * ACT * BLOCK * BLOCK * HD,
            bytes_accessed=10 * 2**20,
            transcendentals=2 * pairs * ACT * BLOCK * BLOCK,
        ),
    )(place, q, mine, other)


def on_device(queries, keys, values, active):
    z, near, y, far = (lax.axis_size(a) for a in CHIP_AXES)
    heads = near * z * y
    blocks = queries.shape[0] // BLOCK
    core, far_id = lax.axis_index("core"), lax.axis_index("far")

    q, kv = pack(queries, keys, values, heads, far, 4)
    kv = kv.reshape(heads * far, 2 * BLOCK, BLOCK)

    q = lax.all_to_all(q, HEAD_AXES, 0, 0, tiled=True)
    mine = lax.all_to_all(kv, CHIP_AXES, 0, 0, tiled=True)
    other = lax.ppermute(mine, "core", [(0, 1), (1, 0)])

    chunks = heads * far
    table = active.reshape(near, z, 2, far, y, blocks, ACT)
    table = lax.dynamic_slice(
        table, (0, 0, core, far_id, 0, 0, 0), (near, z, 1, 1, y, blocks, ACT)
    )
    table = jnp.swapaxes(table, 0, 1).reshape(-1)
    device, half = table // blocks, table % blocks
    chunk = device // (y * far * 2)
    chunk = chunk % z * near + chunk // z
    chunk = (chunk * y + device % y) * far + device // y % far
    chunk = chunk + jnp.where(device // (y * far) % 2 != core, chunks, 0)
    place = jnp.concatenate([chunk + 2 * chunks * half, chunk + 2 * chunks * (1 - half)])

    out = attend(place, q, mine, other)
    out = lax.all_to_all(out, HEAD_AXES, 0, 0, tiled=True)
    return unpack(out, 2)


def solution(mesh):
    fine = Mesh(mesh.devices.reshape(2, 4, 2, 2, 4), AXES)
    tokens = P(AXES, None)
    return jax.shard_map(
        on_device,
        mesh=fine,
        in_specs=(tokens, tokens, tokens, P()),
        out_specs=tokens,
        check_vma=False,
    )
```

```python
import functools
import math

import jax
import jax.numpy as jnp
from jax import lax
from jax.experimental import pallas as pl
from jax.experimental.pallas import tpu as pltpu
from jax.sharding import Mesh, PartitionSpec as P

HD = 64
BLOCK = 128
ACT = 24
LIMIT = 2.0**100
KEY_COPIES = 4

AXES = ("near", "z", "core", "far", "y")
HEAD_AXES = ("z", "near", "y")
CHIP_AXES = ("z", "near", "y", "far")


def swap_halves(x):
    half = x.shape[1] // 2
    return jnp.concatenate([x[:, half:], x[:, :half]], axis=1)


def both_blocks(x):
    low = lax.broadcasted_iota(jnp.int32, (BLOCK, 2 * HD), 1) < HD
    top, bottom = x[:BLOCK], x[BLOCK:]
    return jnp.where(low, top, swap_halves(bottom)), jnp.where(low, swap_halves(top), bottom)


def pack_kernel(q_ref, k_ref, v_ref, q_out, kv_out, q, k, v, q_new, kv_new, came, gone):
    heads, copies = kv_out.shape[:2]
    parts = came.shape[0]
    width = q.shape[1] // parts
    share = heads // parts
    arrivals = []
    for part in range(parts):
        columns = pl.ds(part * width, width)
        arrivals.append(
            [
                pltpu.make_async_copy(there.at[:, columns], here.at[:, columns], came.at[part, n])
                for n, (there, here) in enumerate(((k_ref, k), (v_ref, v), (q_ref, q)))
            ]
        )
        for copy in arrivals[part]:
            copy.start()
    departures = []
    for part in range(parts):
        for copy in arrivals[part]:
            copy.wait()
        for pair in range(part * width // (2 * HD), (part + 1) * width // (2 * HD)):
            columns = pl.ds(pair * 2 * HD, 2 * HD)
            keys = both_blocks(k[:, columns])
            queries = both_blocks(q[:, columns])
            values = jnp.transpose(v[:, columns])
            for n in range(2):
                rows = values[n * HD : (n + 1) * HD]
                q_new[2 * pair + n] = queries[n]
                kv_new[2 * pair + n, :BLOCK] = keys[n]
                kv_new[2 * pair + n, BLOCK : BLOCK + HD] = rows[:, :BLOCK]
                kv_new[2 * pair + n, BLOCK + HD :] = rows[:, BLOCK:]
        here = pl.ds(part * share, share)
        for n in range(copies):
            departures.append(
                pltpu.make_async_copy(kv_new.at[here], kv_out.at[here, n], gone.at[part, n])
            )
        departures.append(
            pltpu.make_async_copy(q_new.at[here], q_out.at[here], gone.at[part, copies])
        )
        for copy in departures[-copies - 1 :]:
            copy.start()
    for copy in departures:
        copy.wait()


def pack(queries, keys, values, heads, copies, parts):
    anywhere = pl.BlockSpec(memory_space=pl.ANY)
    whole = pltpu.VMEM(queries.shape, queries.dtype)
    return pl.pallas_call(
        pack_kernel,
        out_shape=(
            jax.ShapeDtypeStruct((heads, BLOCK, 2 * HD), queries.dtype),
            jax.ShapeDtypeStruct((heads, copies, 2 * BLOCK, BLOCK), keys.dtype),
        ),
        in_specs=[anywhere] * 3,
        out_specs=(anywhere, anywhere),
        scratch_shapes=[whole] * 3
        + [
            pltpu.VMEM((heads, BLOCK, 2 * HD), queries.dtype),
            pltpu.VMEM((heads, 2 * BLOCK, BLOCK), keys.dtype),
            pltpu.SemaphoreType.DMA((parts, 3)),
            pltpu.SemaphoreType.DMA((parts, copies + 1)),
        ],
        compiler_params=pltpu.CompilerParams(vmem_limit_bytes=63 * 2**20),
    )(queries, keys, values)


def unpack_kernel(x_ref, o_ref):
    low = lax.broadcasted_iota(jnp.int32, (BLOCK, 2 * HD), 1) < HD
    for pair in range(x_ref.shape[0] // 2):
        columns = pl.ds(pair * 2 * HD, 2 * HD)
        x, y = x_ref[2 * pair], x_ref[2 * pair + 1]
        o_ref[:BLOCK, columns] = jnp.where(low, x, swap_halves(y))
        o_ref[BLOCK:, columns] = jnp.where(low, swap_halves(x), y)


def unpack(x, groups):
    heads = x.shape[0]
    return pl.pallas_call(
        unpack_kernel,
        grid=(groups,),
        out_shape=jax.ShapeDtypeStruct((2 * BLOCK, heads * HD), x.dtype),
        in_specs=[pl.BlockSpec((heads // groups, BLOCK, 2 * HD), lambda g: (g, 0, 0))],
        out_specs=pl.BlockSpec((2 * BLOCK, heads * HD // groups), lambda g: (0, g)),
    )(x)


def attend_kernel(
    place_ref, q_ref, mine_ref, other_ref, o_ref, kk, vt, q2, shift, sums, sems
):
    pairs = q_ref.shape[0]
    chunks = mine_ref.shape[0]
    low = lax.broadcasted_iota(jnp.int32, (BLOCK, BLOCK), 1) < HD

    keys, rest = [], []
    piece = chunks // KEY_COPIES
    for n, ref in enumerate((mine_ref, other_ref)):
        for part in range(KEY_COPIES):
            there, here = pl.ds(part * piece, piece), pl.ds(n * chunks + part * piece, piece)
            copy = pltpu.make_async_copy(
                ref.at[there, :BLOCK, :], kk.at[here], sems.at[n, part]
            )
            keys.append((copy, n * chunks + part * piece))
        for side in range(2):
            here = pl.ds((2 * side + n) * chunks, chunks)
            rows = ref.at[:, BLOCK + side * HD : BLOCK + (side + 1) * HD, :]
            rest.append(
                pltpu.make_async_copy(rows, vt.at[here], sems.at[n, KEY_COPIES + side])
            )
    for copy, _ in keys:
        copy.start()
    for copy in rest:
        copy.start()

    @pl.loop(0, pairs, step=4)
    def _(first):
        for i in [first + u for u in range(4)]:
            q = jnp.transpose(q_ref[i].astype(jnp.float32)).astype(jnp.bfloat16)
            zero = jnp.zeros((HD, BLOCK), jnp.bfloat16)
            q2[i, :HD, :BLOCK] = q[:HD]
            q2[i, :HD, BLOCK:] = zero
            q2[i, HD:, :BLOCK] = zero
            q2[i, HD:, BLOCK:] = q[HD:]

    for copy, begin in keys:
        copy.wait()

        @pl.loop(begin, begin + piece, step=8)
        def _(first):
            for c in [first + u for u in range(8)]:
                kk[2 * chunks + c] = swap_halves(kk[c])

    def scores(i, t, n):
        rows = []
        for j in range(n):
            a = place_ref[2 * i * ACT + t + j]
            b = place_ref[(2 * (pairs + i) + 1) * ACT + t + j]
            rows.append(jnp.where(low, kk[a], kk[b]))
        rows = jnp.concatenate(rows, axis=0) if n > 1 else rows[0]
        return jnp.dot(rows, q2[i], preferred_element_type=jnp.float32)

    factor = math.log2(math.e) / math.sqrt(HD)

    @pl.loop(0, pairs, step=8)
    def _(first):
        for i in [first + u for u in range(8)]:
            shift[i] = factor * jnp.max(scores(i, 0, 1), axis=0, keepdims=True)

    for copy in rest:
        copy.wait()

    def values(i, n, t, count):
        blocks = [vt[place_ref[(2 * i + n) * ACT + t + j]] for j in range(count)]
        return jnp.concatenate(blocks, axis=1)

    def weights(i, s):
        return jnp.exp2(s * factor - shift[i]).astype(jnp.bfloat16)

    def weighted(i, t, w, count):
        ones = jnp.ones((16, count * BLOCK), jnp.bfloat16)
        v = jnp.concatenate([values(i, 0, t, count), values(i, 1, t, count), ones], axis=0)
        return jnp.dot(v, w, preferred_element_type=jnp.float32)

    def finish(i, total):
        sums[i] = total[2 * HD : 2 * HD + 1]
        inverse = 1.0 / sums[i]
        out = jnp.concatenate(
            [
                total[:HD, :BLOCK] * inverse[:, :BLOCK],
                total[HD : 2 * HD, BLOCK:] * inverse[:, BLOCK:],
            ],
            axis=0,
        )
        o_ref[i] = jnp.transpose(out).astype(jnp.bfloat16)

    def run(todo, count):
        steps = [(i, t) for i in todo for t in range(0, ACT, count)]
        score, weight, total = {}, {}, None
        for k in range(len(steps) + 2):
            if k < len(steps):
                score[k] = scores(*steps[k], count)
            if 0 < k <= len(steps):
                weight[k - 1] = weights(steps[k - 1][0], score.pop(k - 1))
            if 1 < k:
                i, t = steps[k - 2]
                part = weighted(i, t, weight.pop(k - 2), count)
                total = part if t == 0 else total + part
                if t + count == ACT:
                    finish(i, total)

    @pl.loop(0, pairs, step=16)
    def _(first):
        run([first + u for u in range(16)], 4)

    def lost(s):
        return jnp.max(jnp.where(s <= LIMIT, 0.0, 1.0)) > 0.0

    @pl.when(lost(sums[...]))
    def _():
        @pl.loop(0, pairs)
        def _(i):
            @pl.when(lost(sums[i]))
            def _():
                def higher(t, top):
                    return jnp.maximum(top, jnp.max(scores(i, t, 1), axis=0, keepdims=True))

                lowest = jnp.full((1, 2 * BLOCK), -jnp.inf, jnp.float32)
                shift[i] = factor * lax.fori_loop(0, ACT, higher, lowest)
                run([i], 2)


def attend(place, q, mine, other):
    pairs, chunks = q.shape[0], mine.shape[0]
    vmem = pl.BlockSpec(memory_space=pltpu.VMEM)
    anywhere = pl.BlockSpec(memory_space=pl.ANY)
    return pl.pallas_call(
        attend_kernel,
        out_shape=jax.ShapeDtypeStruct(q.shape, jnp.bfloat16),
        in_specs=[pl.BlockSpec(memory_space=pltpu.SMEM), vmem, anywhere, anywhere],
        out_specs=vmem,
        scratch_shapes=[
            pltpu.VMEM((4 * chunks, BLOCK, BLOCK), jnp.bfloat16),
            pltpu.VMEM((4 * chunks, HD, BLOCK), jnp.bfloat16),
            pltpu.VMEM((pairs, BLOCK, 2 * BLOCK), jnp.bfloat16),
            pltpu.VMEM((pairs, 1, 2 * BLOCK), jnp.float32),
            pltpu.VMEM((pairs, 1, 2 * BLOCK), jnp.float32),
            pltpu.SemaphoreType.DMA((2, KEY_COPIES + 2)),
        ],
        compiler_params=pltpu.CompilerParams(vmem_limit_bytes=48 * 2**20),
        cost_estimate=pl.CostEstimate(
            flops=8 * pairs * ACT * BLOCK * BLOCK * HD,
            bytes_accessed=10 * 2**20,
            transcendentals=2 * pairs * ACT * BLOCK * BLOCK,
        ),
    )(place, q, mine, other)


def on_device(queries, keys, values, active):
    z, near, y, far = (lax.axis_size(a) for a in CHIP_AXES)
    heads = near * z * y
    blocks = queries.shape[0] // BLOCK
    core, far_id = lax.axis_index("core"), lax.axis_index("far")

    q, kv = pack(queries, keys, values, heads, far, 4)
    kv = kv.reshape(heads * far, 2 * BLOCK, BLOCK)

    q = lax.all_to_all(q, HEAD_AXES, 0, 0, tiled=True)
    mine = lax.all_to_all(kv, CHIP_AXES, 0, 0, tiled=True)
    other = lax.ppermute(mine, "core", [(0, 1), (1, 0)])

    chunks = heads * far
    table = active.reshape(near, z, 2, far, y, blocks, ACT)
    table = lax.dynamic_slice(
        table, (0, 0, core, far_id, 0, 0, 0), (near, z, 1, 1, y, blocks, ACT)
    )
    table = jnp.swapaxes(table, 0, 1).reshape(-1)
    device, half = table // blocks, table % blocks
    chunk = device // (y * far * 2)
    chunk = chunk % z * near + chunk // z
    chunk = (chunk * y + device % y) * far + device // y % far
    chunk = chunk + jnp.where(device // (y * far) % 2 != core, chunks, 0)
    place = jnp.concatenate([chunk + 2 * chunks * half, chunk + 2 * chunks * (1 - half)])

    out = attend(place, q, mine, other)
    out = lax.all_to_all(out, HEAD_AXES, 0, 0, tiled=True)
    return unpack(out, 2)


def solution(mesh):
    fine = Mesh(mesh.devices.reshape(2, 4, 2, 2, 4), AXES)
    tokens = P(AXES, None)
    return jax.shard_map(
        on_device,
        mesh=fine,
        in_specs=(tokens, tokens, tokens, P()),
        out_specs=tokens,
        check_vma=False,
    )
```

```python
import functools
import math

import jax
import jax.numpy as jnp
from jax import lax
from jax.experimental import pallas as pl
from jax.experimental.pallas import tpu as pltpu
from jax.sharding import Mesh, PartitionSpec as P

HD = 64
BLOCK = 128
ACT = 24
LIMIT = 2.0**100
KEY_COPIES = 4

AXES = ("near", "z", "core", "far", "y")
HEAD_AXES = ("near", "z", "y")
CHIP_AXES = ("near", "z", "y", "far")


def swap_halves(x):
    half = x.shape[1] // 2
    return jnp.concatenate([x[:, half:], x[:, :half]], axis=1)


def both_blocks(x):
    low = lax.broadcasted_iota(jnp.int32, (BLOCK, 2 * HD), 1) < HD
    top, bottom = x[:BLOCK], x[BLOCK:]
    return jnp.where(low, top, swap_halves(bottom)), jnp.where(low, swap_halves(top), bottom)


def pack_kernel(q_ref, k_ref, v_ref, q_out, kv_out, q, k, v, q_new, kv_new, came, gone):
    heads, copies = kv_out.shape[:2]
    parts = came.shape[0]
    width = q.shape[1] // parts
    share = heads // parts
    arrivals = []
    for part in range(parts):
        columns = pl.ds(part * width, width)
        arrivals.append(
            [
                pltpu.make_async_copy(there.at[:, columns], here.at[:, columns], came.at[part, n])
                for n, (there, here) in enumerate(((k_ref, k), (v_ref, v), (q_ref, q)))
            ]
        )
        for copy in arrivals[part]:
            copy.start()
    departures = []
    for part in range(parts):
        for copy in arrivals[part]:
            copy.wait()
        for pair in range(part * width // (2 * HD), (part + 1) * width // (2 * HD)):
            columns = pl.ds(pair * 2 * HD, 2 * HD)
            keys = both_blocks(k[:, columns])
            queries = both_blocks(q[:, columns])
            values = jnp.transpose(v[:, columns])
            for n in range(2):
                rows = values[n * HD : (n + 1) * HD]
                q_new[2 * pair + n] = queries[n]
                kv_new[2 * pair + n, :BLOCK] = keys[n]
                kv_new[2 * pair + n, BLOCK : BLOCK + HD] = rows[:, :BLOCK]
                kv_new[2 * pair + n, BLOCK + HD :] = rows[:, BLOCK:]
        here = pl.ds(part * share, share)
        for n in range(copies):
            departures.append(
                pltpu.make_async_copy(kv_new.at[here], kv_out.at[here, n], gone.at[part, n])
            )
        departures.append(
            pltpu.make_async_copy(q_new.at[here], q_out.at[here], gone.at[part, copies])
        )
        for copy in departures[-copies - 1 :]:
            copy.start()
    for copy in departures:
        copy.wait()


def pack(queries, keys, values, heads, copies, parts):
    anywhere = pl.BlockSpec(memory_space=pl.ANY)
    whole = pltpu.VMEM(queries.shape, queries.dtype)
    return pl.pallas_call(
        pack_kernel,
        out_shape=(
            jax.ShapeDtypeStruct((heads, BLOCK, 2 * HD), queries.dtype),
            jax.ShapeDtypeStruct((heads, copies, 2 * BLOCK, BLOCK), keys.dtype),
        ),
        in_specs=[anywhere] * 3,
        out_specs=(anywhere, anywhere),
        scratch_shapes=[whole] * 3
        + [
            pltpu.VMEM((heads, BLOCK, 2 * HD), queries.dtype),
            pltpu.VMEM((heads, 2 * BLOCK, BLOCK), keys.dtype),
            pltpu.SemaphoreType.DMA((parts, 3)),
            pltpu.SemaphoreType.DMA((parts, copies + 1)),
        ],
        compiler_params=pltpu.CompilerParams(vmem_limit_bytes=63 * 2**20),
    )(queries, keys, values)


def unpack_kernel(x_ref, o_ref):
    low = lax.broadcasted_iota(jnp.int32, (BLOCK, 2 * HD), 1) < HD
    for pair in range(x_ref.shape[0] // 2):
        columns = pl.ds(pair * 2 * HD, 2 * HD)
        x, y = x_ref[2 * pair], x_ref[2 * pair + 1]
        o_ref[:BLOCK, columns] = jnp.where(low, x, swap_halves(y))
        o_ref[BLOCK:, columns] = jnp.where(low, swap_halves(x), y)


def unpack(x, groups):
    heads = x.shape[0]
    return pl.pallas_call(
        unpack_kernel,
        grid=(groups,),
        out_shape=jax.ShapeDtypeStruct((2 * BLOCK, heads * HD), x.dtype),
        in_specs=[pl.BlockSpec((heads // groups, BLOCK, 2 * HD), lambda g: (g, 0, 0))],
        out_specs=pl.BlockSpec((2 * BLOCK, heads * HD // groups), lambda g: (0, g)),
    )(x)


def attend_kernel(
    place_ref, q_ref, mine_ref, other_ref, o_ref, kk, vt, q2, shift, sums, sems
):
    pairs = q_ref.shape[0]
    chunks = mine_ref.shape[0]
    low = lax.broadcasted_iota(jnp.int32, (BLOCK, BLOCK), 1) < HD

    keys, rest = [], []
    piece = chunks // KEY_COPIES
    for n, ref in enumerate((mine_ref, other_ref)):
        for part in range(KEY_COPIES):
            there, here = pl.ds(part * piece, piece), pl.ds(n * chunks + part * piece, piece)
            copy = pltpu.make_async_copy(
                ref.at[there, :BLOCK, :], kk.at[here], sems.at[n, part]
            )
            keys.append((copy, n * chunks + part * piece))
        for side in range(2):
            here = pl.ds((2 * side + n) * chunks, chunks)
            rows = ref.at[:, BLOCK + side * HD : BLOCK + (side + 1) * HD, :]
            rest.append(
                pltpu.make_async_copy(rows, vt.at[here], sems.at[n, KEY_COPIES + side])
            )
    for copy, _ in keys:
        copy.start()
    for copy in rest:
        copy.start()

    @pl.loop(0, pairs, step=8)
    def _(first):
        for i in [first + u for u in range(8)]:
            q = jnp.transpose(q_ref[i].astype(jnp.float32)).astype(jnp.bfloat16)
            zero = jnp.zeros((HD, BLOCK), jnp.bfloat16)
            q2[i, :HD, :BLOCK] = q[:HD]
            q2[i, :HD, BLOCK:] = zero
            q2[i, HD:, :BLOCK] = zero
            q2[i, HD:, BLOCK:] = q[HD:]

    for copy, begin in keys:
        copy.wait()

        @pl.loop(begin, begin + piece, step=8)
        def _(first):
            for c in [first + u for u in range(8)]:
                kk[2 * chunks + c] = swap_halves(kk[c])

    def scores(i, t, n):
        rows = []
        for j in range(n):
            a = place_ref[2 * i * ACT + t + j]
            b = place_ref[(2 * (pairs + i) + 1) * ACT + t + j]
            rows.append(jnp.where(low, kk[a], kk[b]))
        rows = jnp.concatenate(rows, axis=0) if n > 1 else rows[0]
        return jnp.dot(rows, q2[i], preferred_element_type=jnp.float32)

    factor = math.log2(math.e) / math.sqrt(HD)

    @pl.loop(0, pairs, step=16)
    def _(first):
        for i in [first + u for u in range(16)]:
            shift[i] = factor * jnp.max(scores(i, 0, 1), axis=0, keepdims=True)

    for copy in rest:
        copy.wait()

    def values(i, n, t, count):
        blocks = [vt[place_ref[(2 * i + n) * ACT + t + j]] for j in range(count)]
        return jnp.concatenate(blocks, axis=1)

    def weights(i, s):
        return jnp.exp2(s * factor - shift[i]).astype(jnp.bfloat16)

    def weighted(i, t, w, count):
        ones = jnp.ones((16, count * BLOCK), jnp.bfloat16)
        v = jnp.concatenate([values(i, 0, t, count), values(i, 1, t, count), ones], axis=0)
        return jnp.dot(v, w, preferred_element_type=jnp.float32)

    def finish(i, total):
        sums[i] = total[2 * HD : 2 * HD + 1]
        inverse = 1.0 / sums[i]
        out = jnp.concatenate(
            [
                total[:HD, :BLOCK] * inverse[:, :BLOCK],
                total[HD : 2 * HD, BLOCK:] * inverse[:, BLOCK:],
            ],
            axis=0,
        )
        o_ref[i] = jnp.transpose(out).astype(jnp.bfloat16)

    def run(todo, count):
        steps = [(i, t) for i in todo for t in range(0, ACT, count)]
        score, weight, total = {}, {}, None
        for k in range(len(steps) + 2):
            if k < len(steps):
                score[k] = scores(*steps[k], count)
            if 0 < k <= len(steps):
                weight[k - 1] = weights(steps[k - 1][0], score.pop(k - 1))
            if 1 < k:
                i, t = steps[k - 2]
                part = weighted(i, t, weight.pop(k - 2), count)
                total = part if t == 0 else total + part
                if t + count == ACT:
                    finish(i, total)

    @pl.loop(0, pairs, step=16)
    def _(first):
        run([first + u for u in range(16)], 4)

    def lost(s):
        return jnp.max(jnp.where(s <= LIMIT, 0.0, 1.0)) > 0.0

    @pl.when(lost(sums[...]))
    def _():
        @pl.loop(0, pairs)
        def _(i):
            @pl.when(lost(sums[i]))
            def _():
                def higher(t, top):
                    return jnp.maximum(top, jnp.max(scores(i, t, 1), axis=0, keepdims=True))

                lowest = jnp.full((1, 2 * BLOCK), -jnp.inf, jnp.float32)
                shift[i] = factor * lax.fori_loop(0, ACT, higher, lowest)
                run([i], 2)


def attend(place, q, mine, other):
    pairs, chunks = q.shape[0], mine.shape[0]
    vmem = pl.BlockSpec(memory_space=pltpu.VMEM)
    anywhere = pl.BlockSpec(memory_space=pl.ANY)
    return pl.pallas_call(
        attend_kernel,
        out_shape=jax.ShapeDtypeStruct(q.shape, jnp.bfloat16),
        in_specs=[pl.BlockSpec(memory_space=pltpu.SMEM), vmem, anywhere, anywhere],
        out_specs=vmem,
        scratch_shapes=[
            pltpu.VMEM((4 * chunks, BLOCK, BLOCK), jnp.bfloat16),
            pltpu.VMEM((4 * chunks, HD, BLOCK), jnp.bfloat16),
            pltpu.VMEM((pairs, BLOCK, 2 * BLOCK), jnp.bfloat16),
            pltpu.VMEM((pairs, 1, 2 * BLOCK), jnp.float32),
            pltpu.VMEM((pairs, 1, 2 * BLOCK), jnp.float32),
            pltpu.SemaphoreType.DMA((2, KEY_COPIES + 2)),
        ],
        compiler_params=pltpu.CompilerParams(vmem_limit_bytes=48 * 2**20),
        cost_estimate=pl.CostEstimate(
            flops=8 * pairs * ACT * BLOCK * BLOCK * HD,
            bytes_accessed=10 * 2**20,
            transcendentals=2 * pairs * ACT * BLOCK * BLOCK,
        ),
    )(place, q, mine, other)


def on_device(queries, keys, values, active):
    near, z, y, far = (lax.axis_size(a) for a in CHIP_AXES)
    heads = near * z * y
    blocks = queries.shape[0] // BLOCK
    core, far_id = lax.axis_index("core"), lax.axis_index("far")

    q, kv = pack(queries, keys, values, heads, far, 4)
    kv = kv.reshape(heads * far, 2 * BLOCK, BLOCK)

    q = lax.all_to_all(q, HEAD_AXES, 0, 0, tiled=True)
    mine = lax.all_to_all(kv, CHIP_AXES, 0, 0, tiled=True)
    other = lax.ppermute(mine, "core", [(0, 1), (1, 0)])

    chunks = heads * far
    table = active.reshape(near, z, 2, far, y, blocks, ACT)
    table = lax.dynamic_slice(
        table, (0, 0, core, far_id, 0, 0, 0), (near, z, 1, 1, y, blocks, ACT)
    ).reshape(-1)
    device, half = table // blocks, table % blocks
    chunk = (device // (y * far * 2) * y + device % y) * far + device // y % far
    chunk = chunk + jnp.where(device // (y * far) % 2 != core, chunks, 0)
    place = jnp.concatenate([chunk + 2 * chunks * half, chunk + 2 * chunks * (1 - half)])

    out = attend(place, q, mine, other)
    out = lax.all_to_all(out, HEAD_AXES, 0, 0, tiled=True)
    return unpack(out, 2)


def solution(mesh):
    fine = Mesh(mesh.devices.reshape(2, 4, 2, 2, 4), AXES)
    tokens = P(AXES, None)
    return jax.shard_map(
        on_device,
        mesh=fine,
        in_specs=(tokens, tokens, tokens, P()),
        out_specs=tokens,
        check_vma=False,
    )
```

```python
import functools
import math

import jax
import jax.numpy as jnp
from jax import lax
from jax.experimental import pallas as pl
from jax.experimental.pallas import tpu as pltpu
from jax.sharding import Mesh, PartitionSpec as P

HD = 64
BLOCK = 128
ACT = 24
LIMIT = 2.0**100
KEY_COPIES = 4

AXES = ("near", "z", "core", "far", "y")
HEAD_AXES = ("near", "z", "y")
CHIP_AXES = ("near", "z", "y", "far")


def swap_halves(x):
    half = x.shape[1] // 2
    return jnp.concatenate([x[:, half:], x[:, :half]], axis=1)


def both_blocks(x):
    low = lax.broadcasted_iota(jnp.int32, (BLOCK, 2 * HD), 1) < HD
    top, bottom = x[:BLOCK], x[BLOCK:]
    return jnp.where(low, top, swap_halves(bottom)), jnp.where(low, swap_halves(top), bottom)


def pack_kernel(q_ref, k_ref, v_ref, q_out, kv_out, q, k, v, q_new, kv_new, came, gone):
    heads, copies = kv_out.shape[:2]
    parts = came.shape[0]
    width = q.shape[1] // parts
    share = heads // parts
    arrivals = []
    for part in range(parts):
        columns = pl.ds(part * width, width)
        arrivals.append(
            [
                pltpu.make_async_copy(there.at[:, columns], here.at[:, columns], came.at[part, n])
                for n, (there, here) in enumerate(((k_ref, k), (v_ref, v), (q_ref, q)))
            ]
        )
        for copy in arrivals[part]:
            copy.start()
    departures = []
    for part in range(parts):
        for copy in arrivals[part]:
            copy.wait()
        for pair in range(part * width // (2 * HD), (part + 1) * width // (2 * HD)):
            columns = pl.ds(pair * 2 * HD, 2 * HD)
            keys = both_blocks(k[:, columns])
            queries = both_blocks(q[:, columns])
            values = jnp.transpose(v[:, columns])
            for n in range(2):
                rows = values[n * HD : (n + 1) * HD]
                q_new[2 * pair + n] = queries[n]
                kv_new[2 * pair + n, :BLOCK] = keys[n]
                kv_new[2 * pair + n, BLOCK : BLOCK + HD] = rows[:, :BLOCK]
                kv_new[2 * pair + n, BLOCK + HD :] = rows[:, BLOCK:]
        here = pl.ds(part * share, share)
        for n in range(copies):
            departures.append(
                pltpu.make_async_copy(kv_new.at[here], kv_out.at[here, n], gone.at[part, n])
            )
        departures.append(
            pltpu.make_async_copy(q_new.at[here], q_out.at[here], gone.at[part, copies])
        )
        for copy in departures[-copies - 1 :]:
            copy.start()
    for copy in departures:
        copy.wait()


def pack(queries, keys, values, heads, copies, parts):
    anywhere = pl.BlockSpec(memory_space=pl.ANY)
    whole = pltpu.VMEM(queries.shape, queries.dtype)
    return pl.pallas_call(
        pack_kernel,
        out_shape=(
            jax.ShapeDtypeStruct((heads, BLOCK, 2 * HD), queries.dtype),
            jax.ShapeDtypeStruct((heads, copies, 2 * BLOCK, BLOCK), keys.dtype),
        ),
        in_specs=[anywhere] * 3,
        out_specs=(anywhere, anywhere),
        scratch_shapes=[whole] * 3
        + [
            pltpu.VMEM((heads, BLOCK, 2 * HD), queries.dtype),
            pltpu.VMEM((heads, 2 * BLOCK, BLOCK), keys.dtype),
            pltpu.SemaphoreType.DMA((parts, 3)),
            pltpu.SemaphoreType.DMA((parts, copies + 1)),
        ],
        compiler_params=pltpu.CompilerParams(vmem_limit_bytes=63 * 2**20),
    )(queries, keys, values)


def unpack_kernel(x_ref, o_ref):
    low = lax.broadcasted_iota(jnp.int32, (BLOCK, 2 * HD), 1) < HD
    for pair in range(x_ref.shape[0] // 2):
        columns = pl.ds(pair * 2 * HD, 2 * HD)
        x, y = x_ref[2 * pair], x_ref[2 * pair + 1]
        o_ref[:BLOCK, columns] = jnp.where(low, x, swap_halves(y))
        o_ref[BLOCK:, columns] = jnp.where(low, swap_halves(x), y)


def unpack(x, groups):
    heads = x.shape[0]
    return pl.pallas_call(
        unpack_kernel,
        grid=(groups,),
        out_shape=jax.ShapeDtypeStruct((2 * BLOCK, heads * HD), x.dtype),
        in_specs=[pl.BlockSpec((heads // groups, BLOCK, 2 * HD), lambda g: (g, 0, 0))],
        out_specs=pl.BlockSpec((2 * BLOCK, heads * HD // groups), lambda g: (0, g)),
    )(x)


def attend_kernel(
    place_ref, q_ref, mine_ref, other_ref, o_ref, kk, vt, q2, shift, sums, sems
):
    pairs = q_ref.shape[0]
    chunks = mine_ref.shape[0]
    low = lax.broadcasted_iota(jnp.int32, (BLOCK, BLOCK), 1) < HD

    keys, rest = [], []
    piece = chunks // KEY_COPIES
    for n, ref in enumerate((mine_ref, other_ref)):
        for part in range(KEY_COPIES):
            there, here = pl.ds(part * piece, piece), pl.ds(n * chunks + part * piece, piece)
            copy = pltpu.make_async_copy(
                ref.at[there, :BLOCK, :], kk.at[here], sems.at[n, part]
            )
            keys.append((copy, n * chunks + part * piece))
        for side in range(2):
            here = pl.ds((2 * side + n) * chunks, chunks)
            rows = ref.at[:, BLOCK + side * HD : BLOCK + (side + 1) * HD, :]
            rest.append(
                pltpu.make_async_copy(rows, vt.at[here], sems.at[n, KEY_COPIES + side])
            )
    for copy, _ in keys:
        copy.start()
    for copy in rest:
        copy.start()

    @pl.loop(0, pairs, step=8)
    def _(first):
        for i in [first + u for u in range(8)]:
            q = jnp.transpose(q_ref[i].astype(jnp.float32)).astype(jnp.bfloat16)
            zero = jnp.zeros((HD, BLOCK), jnp.bfloat16)
            q2[i, :HD, :BLOCK] = q[:HD]
            q2[i, :HD, BLOCK:] = zero
            q2[i, HD:, :BLOCK] = zero
            q2[i, HD:, BLOCK:] = q[HD:]

    for copy, begin in keys:
        copy.wait()

        @pl.loop(begin, begin + piece, step=8)
        def _(first):
            for c in [first + u for u in range(8)]:
                kk[2 * chunks + c] = swap_halves(kk[c])

    def scores(i, t, n):
        rows = []
        for j in range(n):
            a = place_ref[2 * i * ACT + t + j]
            b = place_ref[(2 * (pairs + i) + 1) * ACT + t + j]
            rows.append(jnp.where(low, kk[a], kk[b]))
        rows = jnp.concatenate(rows, axis=0) if n > 1 else rows[0]
        return jnp.dot(rows, q2[i], preferred_element_type=jnp.float32)

    factor = math.log2(math.e) / math.sqrt(HD)

    @pl.loop(0, pairs, step=16)
    def _(first):
        for i in [first + u for u in range(16)]:
            shift[i] = factor * jnp.max(scores(i, 0, 1), axis=0, keepdims=True)

    for copy in rest:
        copy.wait()

    def values(i, n, t, count):
        blocks = [vt[place_ref[(2 * i + n) * ACT + t + j]] for j in range(count)]
        return jnp.concatenate(blocks, axis=1)

    def weights(i, s):
        return jnp.exp2(s * factor - shift[i]).astype(jnp.bfloat16)

    def weighted(i, t, w, count):
        ones = jnp.ones((16, count * BLOCK), jnp.bfloat16)
        v = jnp.concatenate([values(i, 0, t, count), values(i, 1, t, count), ones], axis=0)
        return jnp.dot(v, w, preferred_element_type=jnp.float32)

    def finish(i, total):
        sums[i] = total[2 * HD : 2 * HD + 1]
        inverse = 1.0 / sums[i]
        out = jnp.concatenate(
            [
                total[:HD, :BLOCK] * inverse[:, :BLOCK],
                total[HD : 2 * HD, BLOCK:] * inverse[:, BLOCK:],
            ],
            axis=0,
        )
        o_ref[i] = jnp.transpose(out).astype(jnp.bfloat16)

    def run(todo, count):
        steps = [(i, t) for i in todo for t in range(0, ACT, count)]
        score, weight, total = {}, {}, None
        for k in range(len(steps) + 2):
            if k < len(steps):
                score[k] = scores(*steps[k], count)
            if 0 < k <= len(steps):
                weight[k - 1] = weights(steps[k - 1][0], score.pop(k - 1))
            if 1 < k:
                i, t = steps[k - 2]
                part = weighted(i, t, weight.pop(k - 2), count)
                total = part if t == 0 else total + part
                if t + count == ACT:
                    finish(i, total)

    run(range(pairs), 4)

    def lost(s):
        return jnp.max(jnp.where(s <= LIMIT, 0.0, 1.0)) > 0.0

    @pl.when(lost(sums[...]))
    def _():
        @pl.loop(0, pairs)
        def _(i):
            @pl.when(lost(sums[i]))
            def _():
                def higher(t, top):
                    return jnp.maximum(top, jnp.max(scores(i, t, 1), axis=0, keepdims=True))

                lowest = jnp.full((1, 2 * BLOCK), -jnp.inf, jnp.float32)
                shift[i] = factor * lax.fori_loop(0, ACT, higher, lowest)
                run([i], 2)


def attend(place, q, mine, other):
    pairs, chunks = q.shape[0], mine.shape[0]
    vmem = pl.BlockSpec(memory_space=pltpu.VMEM)
    anywhere = pl.BlockSpec(memory_space=pl.ANY)
    return pl.pallas_call(
        attend_kernel,
        out_shape=jax.ShapeDtypeStruct(q.shape, jnp.bfloat16),
        in_specs=[pl.BlockSpec(memory_space=pltpu.SMEM), vmem, anywhere, anywhere],
        out_specs=vmem,
        scratch_shapes=[
            pltpu.VMEM((4 * chunks, BLOCK, BLOCK), jnp.bfloat16),
            pltpu.VMEM((4 * chunks, HD, BLOCK), jnp.bfloat16),
            pltpu.VMEM((pairs, BLOCK, 2 * BLOCK), jnp.bfloat16),
            pltpu.VMEM((pairs, 1, 2 * BLOCK), jnp.float32),
            pltpu.VMEM((pairs, 1, 2 * BLOCK), jnp.float32),
            pltpu.SemaphoreType.DMA((2, KEY_COPIES + 2)),
        ],
        compiler_params=pltpu.CompilerParams(vmem_limit_bytes=48 * 2**20),
        cost_estimate=pl.CostEstimate(
            flops=8 * pairs * ACT * BLOCK * BLOCK * HD,
            bytes_accessed=10 * 2**20,
            transcendentals=2 * pairs * ACT * BLOCK * BLOCK,
        ),
    )(place, q, mine, other)


def on_device(queries, keys, values, active):
    near, z, y, far = (lax.axis_size(a) for a in CHIP_AXES)
    heads = near * z * y
    blocks = queries.shape[0] // BLOCK
    core, far_id = lax.axis_index("core"), lax.axis_index("far")

    q, kv = pack(queries, keys, values, heads, far, 4)
    kv = kv.reshape(heads * far, 2 * BLOCK, BLOCK)

    q = lax.all_to_all(q, HEAD_AXES, 0, 0, tiled=True)
    mine = lax.all_to_all(kv, CHIP_AXES, 0, 0, tiled=True)
    other = lax.ppermute(mine, "core", [(0, 1), (1, 0)])

    chunks = heads * far
    table = active.reshape(near, z, 2, far, y, blocks, ACT)
    table = lax.dynamic_slice(
        table, (0, 0, core, far_id, 0, 0, 0), (near, z, 1, 1, y, blocks, ACT)
    ).reshape(-1)
    device, half = table // blocks, table % blocks
    chunk = (device // (y * far * 2) * y + device % y) * far + device // y % far
    chunk = chunk + jnp.where(device // (y * far) % 2 != core, chunks, 0)
    place = jnp.concatenate([chunk + 2 * chunks * half, chunk + 2 * chunks * (1 - half)])

    out = attend(place, q, mine, other)
    out = lax.all_to_all(out, HEAD_AXES, 0, 0, tiled=True)
    return unpack(out, 2)


def solution(mesh):
    fine = Mesh(mesh.devices.reshape(2, 4, 2, 2, 4), AXES)
    tokens = P(AXES, None)
    return jax.shard_map(
        on_device,
        mesh=fine,
        in_specs=(tokens, tokens, tokens, P()),
        out_specs=tokens,
        check_vma=False,
    )
```
